128 devices in a mesh: dp: 8 (over y, x_lo), seq: 16 (over z, x_hi, core).
Axes of the slice: x: 4 (x_hi: 2, x_lo: 2; x = x_hi * 2 + x_lo), y: 4, z: 4, core: 2. Of those that a mesh axis runs over, the one named last changes fastest.
Arguments:
- query_rows: bfloat16 [8, 16, 128, 8192], P('dp', 'seq'), may hold values from -6 to 6
- key_rows: bfloat16 [8, 16, 128, 1024], P('dp', 'seq'), may hold values from -6 to 6
- value_rows: bfloat16 [8, 16, 128, 1024], P('dp', 'seq'), may hold values from -6 to 6
- grad_out: bfloat16 [8, 16, 128, 8192], P('dp', 'seq'), may hold values from -6 to 6
- doc_length: int32 [64], replicated, may hold values from 0 to 1024, as said below
- source_group: int32 [64], replicated, may hold values from 0 to 7
- source_offset: int32 [64], replicated, may hold values from 0 to 1792, as said below
- target_group: int32 [64], replicated, may hold values from 0 to 7, as said below
- target_offset: int32 [64], replicated, may hold values from 0 to 1792, as said below
Outputs:
- grad_query: bfloat16 [8, 16, 128, 8192], P('dp', 'seq')
- grad_key: bfloat16 [8, 16, 128, 1024], P('dp', 'seq')
- grad_value: bfloat16 [8, 16, 128, 1024], P('dp', 'seq')
The draws below stay inside these ranges and needn't reach their ends.
Inputs may be any that keep to these rules, and one draw needn't show every extreme that they name: `doc_length`: entries 4 j to 4 j + 3 describe half j % 2 of source group j // 2, the positions from (j % 2) * 1024 to (j % 2 + 1) * 1024 - 1, which its nonempty entries fill exactly in entry order. Entries of length 0 are empty and have group and offsets 0. Every length is a multiple of 16; a nonempty one has 256 to 1024 positions. `source_offset`: A multiple of 16. `target_group`: all documents of one source half go to one group. The half of source group g whose lengths have the larger sum of squares (the first half on a tie) stays in group g; the other half goes to group p(g), where p is a permutation of the groups with p(g) != g for every g. Every group's new packing is filled exactly, in some order. `target_offset`: A multiple of 16.
All inputs are finite; a program needn't handle non-finite values.
Results may differ from the reference program's by a relative error of at most 0.012.
Values may be sent and summed in bfloat16 or wider, within the bound.
No kernel may reach another device: no remote copies, remote signals or barrier semaphores. Data moves between devices by JAX's collectives and lax.ppermute only.
A program may use at most 128 MiB of HBM per device.

```python
import math
import jax
import jax.numpy as jnp
from jax import lax

QH = 64
KVH = 8
HD = 128
TOK_DEV = 128
N_DP = 8
N_SEQ = 16


def group_cycle(key):
    if N_DP >= 3:
        head_labels = [0, 1, 1 + N_DP // 2]
    else:
        head_labels = [0, 1]
    remaining = [label for label in range(N_DP) if label not in head_labels]
    head_array = jnp.array(head_labels, dtype=jnp.int32)
    if len(remaining) > 0:
        tail_array = jax.random.permutation(key, jnp.array(remaining, dtype=jnp.int32))
        cycle_order = jnp.concatenate([head_array, tail_array])
    else:
        cycle_order = head_array
    return jnp.zeros((N_DP,), jnp.int32).at[cycle_order].set(jnp.roll(cycle_order, -1))


def layout_plan(key):
    halves = 2 * N_DP
    half_units = TOK_DEV // 2
    quarter = half_units // 4
    subkeys = jax.random.split(key, 7)
    half_kind = jax.random.randint(subkeys[0], (halves,), 0, 3)
    single_half = 2 * jax.random.randint(subkeys[1], (), 0, N_DP)
    many_half = 2 * jax.random.randint(subkeys[2], (), 0, N_DP) + 1
    half_index = jnp.arange(halves, dtype=jnp.int32)
    half_kind = jnp.where(half_index == single_half, 0, jnp.where(half_index == many_half, 2, half_kind))
    cut_point = jax.random.randint(subkeys[3], (halves,), quarter, 3 * quarter + 1)
    first_len = jnp.where(half_kind == 0, half_units, jnp.where(half_kind == 1, cut_point, quarter))
    second_len = jnp.where(half_kind == 0, 0, jnp.where(half_kind == 1, half_units - cut_point, quarter))
    rest_len = jnp.where(half_kind == 2, quarter, 0)
    lengths = jnp.stack([first_len, second_len, rest_len, rest_len], axis=1).astype(jnp.int32)
    starts = jnp.cumsum(lengths, axis=1) - lengths + (half_index % 2)[:, None] * half_units
    half_cost = jnp.sum(lengths * lengths, axis=1).reshape(N_DP, 2)
    heavy_half = (half_cost[:, 1] > half_cost[:, 0]).astype(jnp.int32)
    labels = jnp.arange(N_DP, dtype=jnp.int32)
    base_cycle = group_cycle(subkeys[5])
    turn = jax.random.randint(subkeys[4], (), 0, N_DP)
    perm = (base_cycle[(labels - turn) % N_DP] + turn) % N_DP
    inverse = jnp.zeros((N_DP,), jnp.int32).at[perm].set(labels)
    owner_group = half_index // 2
    is_heavy = half_index % 2 == heavy_half[owner_group]
    destination = jnp.where(is_heavy, owner_group, perm[owner_group])
    heavy_source = labels
    light_source = inverse[heavy_source]
    heavy_slab = 2 * heavy_source + heavy_half[heavy_source]
    light_slab = 2 * light_source + 1 - heavy_half[light_source]
    arriving = jnp.concatenate([lengths[heavy_slab], lengths[light_slab]], axis=1)
    sort_keys = jax.random.randint(subkeys[6], (N_DP, 8), 0, 1 << 20) * 8 + jnp.arange(8, dtype=jnp.int32)[None, :]
    many_dest = destination[many_half]
    many_slot = jnp.where(is_heavy[many_half], 0, 4) + 3
    sort_keys = sort_keys.at[many_dest, many_slot].set((1 << 20) * 8)
    sorted_slot = jnp.argsort(sort_keys, axis=1)
    sorted_len = jnp.take_along_axis(arriving, sorted_slot, axis=1)
    sorted_start = jnp.cumsum(sorted_len, axis=1) - sorted_len
    back_slot = jnp.argsort(sorted_slot, axis=1)
    arrive_start = jnp.take_along_axis(sorted_start, back_slot, axis=1)
    entry_base = jnp.where(is_heavy, 0, 4)
    target_start = arrive_start[destination[:, None], entry_base[:, None] + jnp.arange(4, dtype=jnp.int32)[None, :]]
    is_live = lengths > 0
    doc_length = (lengths * N_SEQ).reshape(-1).astype(jnp.int32)
    source_group = jnp.where(is_live, owner_group[:, None], 0).reshape(-1).astype(jnp.int32)
    source_offset = jnp.where(is_live, starts * N_SEQ, 0).reshape(-1).astype(jnp.int32)
    target_group = jnp.where(is_live, destination[:, None], 0).reshape(-1).astype(jnp.int32)
    target_offset = jnp.where(is_live, target_start * N_SEQ, 0).reshape(-1).astype(jnp.int32)
    return (doc_length, source_group, source_offset, target_group, target_offset)


def draw_doc_length(key, part):
    plan_all = layout_plan(key)
    return plan_all[0]


def draw_source_group(key, part):
    plan_all = layout_plan(key)
    return plan_all[1]


def draw_source_offset(key, part):
    plan_all = layout_plan(key)
    return plan_all[2]


def draw_target_group(key, part):
    plan_all = layout_plan(key)
    return plan_all[3]


def draw_target_offset(key, part):
    plan_all = layout_plan(key)
    return plan_all[4]


def draw_query_rows(key, part):
    key = jax.random.fold_in(key, 5)
    shape = (N_DP, N_SEQ, TOK_DEV, QH * HD)
    values = jnp.clip(1.5 * jax.random.normal(key, shape, jnp.float32), -6.0, 6.0)
    return values.astype(jnp.bfloat16)


def draw_key_rows(key, part):
    key = jax.random.fold_in(key, 6)
    shape = (N_DP, N_SEQ, TOK_DEV, KVH * HD)
    values = jnp.clip(jax.random.normal(key, shape, jnp.float32), -6.0, 6.0)
    return values.astype(jnp.bfloat16)


def shard_levels(rng, shape, cuts, least, largest):
    loudness = 1.0
    for axis_at, parts in cuts:
        steps = jax.random.uniform(jax.random.fold_in(jax.random.fold_in(rng, 6), axis_at), (parts,), jnp.float32, least / len(cuts), largest / len(cuts))
        loudness = loudness * jnp.repeat(jnp.exp(steps), shape[axis_at] // parts).reshape((-1,) + (1,) * (len(shape) - 1 - axis_at))
    return loudness


def noise(stream_key, shape, deviation, reach, cuts=(), kind=jnp.bfloat16):
    drawn = deviation * jax.random.normal(stream_key, shape, jnp.float32)
    if cuts:
        drawn = drawn * shard_levels(stream_key, shape, cuts, -0.22, 0.18)
    return jnp.clip(drawn, -reach, reach).astype(kind)


def setup_inputs(seed: int = 0) -> dict:
    seeds = jax.random.split(jax.random.key(seed), 10)
    query_rows = draw_query_rows(jax.random.fold_in(seeds[9], 71), 0)
    key_rows = draw_key_rows(jax.random.fold_in(seeds[9], 71), 0)
    value_rows = noise(seeds[2], (N_DP, N_SEQ, TOK_DEV, KVH * HD), 1.0, 6.0, ((0, 8), (1, 16)))
    grad_out = noise(seeds[3], (N_DP, N_SEQ, TOK_DEV, QH * HD), 1.0, 6.0, ((0, 8), (1, 16)))
    doc_length = draw_doc_length(jax.random.fold_in(seeds[9], 71), 0)
    source_group = draw_source_group(jax.random.fold_in(seeds[9], 71), 0)
    source_offset = draw_source_offset(jax.random.fold_in(seeds[9], 71), 0)
    target_group = draw_target_group(jax.random.fold_in(seeds[9], 71), 0)
    target_offset = draw_target_offset(jax.random.fold_in(seeds[9], 71), 0)
    return {"query_rows": query_rows, "key_rows": key_rows, "value_rows": value_rows, "grad_out": grad_out, "doc_length": doc_length, "source_group": source_group, "source_offset": source_offset, "target_group": target_group, "target_offset": target_offset}


def attend(query_heads, key_one, value_one, grad_heads, starts):
    seq_total, head_count, head_width = query_heads.shape
    inv_root = 1.0 / math.sqrt(head_width)
    block_count = max(1, min(8, seq_total // 512))
    block_rows = seq_total // block_count
    positions = jnp.arange(seq_total, dtype=jnp.int32)
    key_float = key_one.astype(jnp.float32)
    value_float = value_one.astype(jnp.float32)
    key_grad = jnp.zeros((seq_total, head_width), jnp.float32)
    value_grad = jnp.zeros((seq_total, head_width), jnp.float32)
    pieces = []
    for block_id in range(block_count):
        row_start = block_id * block_rows
        row_end = row_start + block_rows
        query_block = query_heads[row_start:row_end].astype(jnp.float32)
        grad_block = grad_heads[row_start:row_end].astype(jnp.float32)
        key_seen = key_float[:row_end]
        value_seen = value_float[:row_end]
        scores = jnp.einsum('qhd,kd->hqk', query_block, key_seen) * inv_root
        allowed = (starts[row_start:row_end, None] == starts[None, :row_end]) & (positions[row_start:row_end, None] >= positions[None, :row_end])
        scores = jnp.where(allowed[None], scores, -jnp.inf)
        row_max = lax.optimization_barrier(jnp.max(scores, axis=2, keepdims=True))
        weights = jnp.exp(scores - row_max)
        softmaxed = weights / lax.optimization_barrier(jnp.sum(weights, axis=2, keepdims=True))
        probs_low = softmaxed.astype(jnp.bfloat16).astype(jnp.float32)
        attended = jnp.einsum('hqk,kd->qhd', probs_low, value_seen).astype(jnp.bfloat16)
        row_delta = lax.optimization_barrier(jnp.sum(attended.astype(jnp.float32) * grad_block, axis=2))
        value_grad = value_grad.at[:row_end].add(jnp.einsum('hqk,qhd->kd', probs_low, grad_block))
        dprobs = jnp.einsum('qhd,kd->hqk', grad_block, value_seen)
        dscores = (softmaxed * (dprobs - jnp.transpose(row_delta)[:, :, None])).astype(jnp.bfloat16).astype(jnp.float32)
        pieces.append((jnp.einsum('hqk,kd->qhd', dscores, key_seen) * inv_root).astype(jnp.bfloat16))
        key_grad = key_grad.at[:row_end].add(jnp.einsum('hqk,qhd->kd', dscores, query_block) * inv_root)
    grad_query = jnp.concatenate(pieces, axis=0).reshape(seq_total, head_count * head_width)
    return (grad_query, key_grad.astype(jnp.bfloat16), value_grad.astype(jnp.bfloat16))

def reference(query_rows, key_rows, value_rows, grad_out, doc_length, source_group, source_offset, target_group, target_offset):
    groups = query_rows.shape[0]
    lanes_count = query_rows.shape[1]
    row_count = query_rows.shape[2]
    seq_total = row_count * lanes_count
    share = QH // KVH

    def flatten(array):
        return jnp.transpose(array, (0, 2, 1, 3)).reshape(groups * seq_total, array.shape[3])

    def restore(array):
        return jnp.transpose(array.reshape(groups, row_count, lanes_count, array.shape[2]), (0, 2, 1, 3))
    positions = jnp.arange(groups * seq_total, dtype=jnp.int32)
    group_of = positions // seq_total
    place = positions % seq_total
    is_live = doc_length > 0
    inside = (target_group[None, :] == group_of[:, None]) & (place[:, None] >= target_offset[None, :]) & (place[:, None] < (target_offset + doc_length)[None, :]) & is_live[None, :]
    inside_hits = inside.astype(jnp.int32)
    source_row = lax.optimization_barrier(jnp.sum(inside_hits * (source_group * seq_total + source_offset - target_offset)[None, :], axis=1)) + place
    starts = lax.optimization_barrier(jnp.sum(inside_hits * target_offset[None, :], axis=1)).reshape(groups, 1, seq_total)
    starts = jnp.broadcast_to(starts, (groups, KVH, seq_total)).reshape(groups * KVH, seq_total)

    def heads_major(array, head_cols):
        placed = flatten(array)[source_row].reshape(groups, seq_total, KVH, head_cols)
        return jnp.transpose(placed, (0, 2, 1, 3)).reshape(groups * KVH, seq_total, head_cols)
    query_items = heads_major(query_rows, share * HD).reshape(groups * KVH, seq_total, share, HD)
    grad_items = heads_major(grad_out, share * HD).reshape(groups * KVH, seq_total, share, HD)
    key_items = heads_major(key_rows, HD)
    value_items = heads_major(value_rows, HD)

    def item_work(item):
        return attend(item[0], item[1], item[2], item[3], item[4])
    grad_query, key_grad, value_grad = lax.map(item_work, (query_items, key_items, value_items, grad_items, starts))

    def group_major(array):
        cols = array.shape[2]
        joined = jnp.transpose(array.reshape(groups, KVH, seq_total, cols), (0, 2, 1, 3))
        return restore(joined.reshape(groups, seq_total, KVH * cols))
    return (group_major(grad_query), group_major(key_grad), group_major(value_grad))
```

```python
import functools
import math

import jax
import jax.numpy as jnp
from jax import lax
from jax.experimental import pallas as pl
from jax.experimental.pallas import tpu as pltpu
from jax.sharding import PartitionSpec as P

QH = 64
KVH = 8
HD = 128
SHARE = QH // KVH
HALF = 64
TILE = 32
CHIPS = 8
WIDTH = SHARE * HD
INV_ROOT = 1.0 / math.sqrt(HD)
LOG2E = 1.4426950408889634
VMEM = 56 * 1024 * 1024

LEN, SRC, TGT, TOFF, ME = 0, 64, 128, 192, 256


def light_half(meta, group):
    stays = jnp.int32(0)
    for i in range(4):
        e = group * 8 + i
        stays = stays | ((meta[LEN + e] > 0) & (meta[TGT + e] == group)).astype(jnp.int32)
    return stays


def half_target(meta, group, half):
    target = jnp.int32(0)
    for i in range(4):
        e = group * 8 + half * 4 + i
        target = jnp.maximum(target, jnp.where(meta[LEN + e] > 0, meta[TGT + e], 0))
    return target


def source_of(meta, group):
    found = jnp.int32(0)
    for other in range(8):
        goes = half_target(meta, other, light_half(meta, other))
        found = found + jnp.where(goes == group, other, 0)
    return found


def pack_first(meta, q_ref, g_ref, k_ref, v_ref, kh_ref, vh_ref, out_ref):
    out_ref[0, :, 0:WIDTH] = q_ref[...]
    out_ref[0, :, WIDTH : 2 * WIDTH] = g_ref[...]
    base = 2 * WIDTH
    out_ref[0, :, base : base + HD] = k_ref[...]
    out_ref[0, :, base + HD : base + 2 * HD] = v_ref[...]
    out_ref[0, :, base + 2 * HD : base + 3 * HD] = kh_ref[...]
    out_ref[0, :, base + 3 * HD : base + 4 * HD] = vh_ref[...]


def pack_second(meta, q_ref, g_ref, out_ref):
    out_ref[0, :, 0:WIDTH] = q_ref[...]
    out_ref[0, :, WIDTH : 2 * WIDTH] = g_ref[...]


def pack(meta, query, grad, key, value):
    def light(m, meta):
        return (light_half(meta, meta[ME]), m)

    def heavy(m, meta):
        return (1 - light_half(meta, meta[ME]), m)

    wide = functools.partial(pl.BlockSpec, (HALF, WIDTH))
    thin = functools.partial(pl.BlockSpec, (HALF, HD))
    first_cols = 2 * WIDTH + 4 * HD
    first = pl.pallas_call(
        pack_first,
        out_shape=jax.ShapeDtypeStruct((CHIPS, HALF, first_cols), jnp.bfloat16),
        grid_spec=pltpu.PrefetchScalarGridSpec(
            num_scalar_prefetch=1,
            grid=(CHIPS,),
            in_specs=[wide(light), wide(light), thin(light), thin(light), thin(heavy), thin(heavy)],
            out_specs=pl.BlockSpec((1, HALF, first_cols), lambda m, meta: (m, 0, 0)),
        ),
        cost_estimate=pl.CostEstimate(flops=0, bytes_accessed=5 << 20, transcendentals=0),
        name="pack_first",
    )(meta, query, grad, key, value, key, value)
    second = pl.pallas_call(
        pack_second,
        out_shape=jax.ShapeDtypeStruct((CHIPS, HALF, 2 * WIDTH), jnp.bfloat16),
        grid_spec=pltpu.PrefetchScalarGridSpec(
            num_scalar_prefetch=1,
            grid=(CHIPS,),
            in_specs=[wide(heavy), wide(heavy)],
            out_specs=pl.BlockSpec((1, HALF, 2 * WIDTH), lambda m, meta: (m, 0, 0)),
        ),
        cost_estimate=pl.CostEstimate(flops=0, bytes_accessed=4 << 20, transcendentals=0),
        name="pack_second",
    )(meta, query, grad)
    return first, second


def attend_kernel(
    is_light,
    meta,
    q_ref,
    g_ref,
    own_ref,
    other_ref,
    dq_ref,
    own_out,
    other_out,
    k_all,
    v_all,
    kt_a,
    kt_b,
    bias_a,
    bias_b,
):
    head = pl.program_id(0)
    tiles = ((0, TILE, kt_a, bias_a), (TILE, HALF, kt_b, bias_b))

    @pl.when(head == 0)
    def _():
        group = meta[ME]
        core = meta[ME + 1] % 2
        half = light_half(meta, group)
        if not is_light:
            half = 1 - half
        k_all[0:CHIPS] = own_ref[:, :, 0:HD]
        k_all[CHIPS : 2 * CHIPS] = other_ref[:, :, 0:HD]
        v_all[0:CHIPS] = own_ref[:, :, HD : 2 * HD]
        v_all[CHIPS : 2 * CHIPS] = other_ref[:, :, HD : 2 * HD]
        own_out[...] = jnp.zeros_like(own_out)
        other_out[...] = jnp.zeros_like(other_out)
        for first, rows, kt, bias in tiles:
            seen = 2 * CHIPS * rows
            kt[...] = k_all[:, 0:rows, :].reshape(seen, HD).T
            queries = CHIPS * TILE
            lane = lax.broadcasted_iota(jnp.int32, (1, queries), 1)
            row_q = lane % TILE + first
            pos_q = row_q * 16 + 2 * (lane // TILE) + core
            start_q = jnp.zeros((1, queries), jnp.int32)
            for i in range(4):
                e = (group * 2 + half) * 4 + i
                length = meta[LEN + e]
                begin = meta[SRC + e] - half * (HALF * 16)
                inside = (row_q * 16 >= begin) & (row_q * 16 < begin + length)
                start_q = jnp.where(inside, begin, start_q)
            sub = lax.broadcasted_iota(jnp.int32, (seen, 1), 0)
            slot = sub // rows
            lane_k = jnp.where(slot < CHIPS, 2 * slot + core, 2 * (slot - CHIPS) + 1 - core)
            pos_k = (sub % rows) * 16 + lane_k
            allowed = (pos_k >= start_q) & (pos_k <= pos_q)
            bias[...] = jnp.where(allowed, 0.0, -1e30)

    for first, rows, kt, bias in tiles:
        seen = 2 * CHIPS * rows
        queries = CHIPS * TILE
        q = q_ref[:, first : first + TILE, :].reshape(queries, HD)
        g = g_ref[:, first : first + TILE, :].reshape(queries, HD)
        k = k_all[:, 0:rows, :].reshape(seen, HD)
        v = v_all[:, 0:rows, :].reshape(seen, HD)
        nt = (((1,), (1,)), ((), ()))
        scores = lax.dot_general(k, q, nt, preferred_element_type=jnp.float32)
        scores = scores * (INV_ROOT * LOG2E) + bias[...]
        top = jnp.max(scores, axis=0, keepdims=True)
        weights = jnp.exp2(scores - top)
        dprobs = lax.dot_general(v, g, nt, preferred_element_type=jnp.float32)
        recip = 1.0 / jnp.sum(weights, axis=0, keepdims=True)
        delta = jnp.sum(weights * dprobs, axis=0, keepdims=True) * recip
        soft = weights * recip
        low = soft.astype(jnp.bfloat16)
        dscores = (soft * (dprobs - delta)).astype(jnp.bfloat16)
        dv = jnp.dot(low, g, preferred_element_type=jnp.float32).reshape(2 * CHIPS, rows, HD)
        dk = jnp.dot(dscores, q, preferred_element_type=jnp.float32).reshape(2 * CHIPS, rows, HD)
        own_out[:, 0:rows, 0:HD] += dk[0:CHIPS]
        own_out[:, 0:rows, HD : 2 * HD] += dv[0:CHIPS]
        other_out[:, 0:rows, 0:HD] += dk[CHIPS : 2 * CHIPS]
        other_out[:, 0:rows, HD : 2 * HD] += dv[CHIPS : 2 * CHIPS]
        dq_t = jnp.dot(kt[...], dscores, preferred_element_type=jnp.float32)
        dq = (dq_t * INV_ROOT).T.astype(jnp.bfloat16).reshape(CHIPS, TILE, HD)
        if is_light:
            dq_ref[0, :, first : first + TILE, :] = dq
        else:
            dq_ref[:, first : first + TILE, :] = dq


def attend(meta, is_light, rows_in, own, own_block, other, other_block):
    if is_light:
        dq_shape = (SHARE, CHIPS, HALF + 16, HD)
        dq_spec = pl.BlockSpec((1, CHIPS, HALF, HD), lambda h, meta: (h, 0, 0, 0))
    else:
        dq_shape = (CHIPS, HALF, WIDTH + 2 * HD)
        dq_spec = pl.BlockSpec((CHIPS, HALF, HD), lambda h, meta: (0, 0, h))
    part = pl.BlockSpec((CHIPS, HALF, 2 * HD), lambda h, meta: (0, 0, 0))
    half = 2 * CHIPS * HALF
    queries = CHIPS * TILE
    return pl.pallas_call(
        functools.partial(attend_kernel, is_light),
        out_shape=(
            jax.ShapeDtypeStruct(dq_shape, jnp.bfloat16),
            jax.ShapeDtypeStruct((CHIPS, HALF, 2 * HD), jnp.float32),
            jax.ShapeDtypeStruct((CHIPS, HALF, 2 * HD), jnp.float32),
        ),
        grid_spec=pltpu.PrefetchScalarGridSpec(
            num_scalar_prefetch=1,
            grid=(SHARE,),
            in_specs=[
                pl.BlockSpec((CHIPS, HALF, HD), lambda h, meta: (0, 0, h)),
                pl.BlockSpec((CHIPS, HALF, HD), lambda h, meta: (0, 0, SHARE + h)),
                pl.BlockSpec((CHIPS, HALF, 2 * HD), lambda h, meta: (0, 0, own_block)),
                pl.BlockSpec((CHIPS, HALF, 2 * HD), lambda h, meta: (0, 0, other_block)),
            ],
            out_specs=(dq_spec, part, part),
            scratch_shapes=[
                pltpu.VMEM((2 * CHIPS, HALF, HD), jnp.bfloat16),
                pltpu.VMEM((2 * CHIPS, HALF, HD), jnp.bfloat16),
                pltpu.VMEM((HD, half // 2), jnp.bfloat16),
                pltpu.VMEM((HD, half), jnp.bfloat16),
                pltpu.VMEM((half // 2, queries), jnp.float32),
                pltpu.VMEM((half, queries), jnp.float32),
            ],
        ),
        compiler_params=pltpu.CompilerParams(vmem_limit_bytes=VMEM),
        cost_estimate=pl.CostEstimate(
            flops=8 << 30, bytes_accessed=6 << 20, transcendentals=3 << 20
        ),
        name="attend_light" if is_light else "attend_heavy",
    )(meta, rows_in, rows_in, own, other)


def join_kernel(is_light, held_ref, mine_ref, came_ref, out_ref):
    total = mine_ref[...] + came_ref[...]
    dk = (total[:, :, 0:HD] * INV_ROOT).astype(jnp.bfloat16)
    dv = total[:, :, HD : 2 * HD].astype(jnp.bfloat16)
    if is_light:
        for j in range(4):
            out_ref[j] = dk[:, 16 * j : 16 * j + 16, :]
            out_ref[4 + j] = dv[:, 16 * j : 16 * j + 16, :]
    else:
        out_ref[:, :, 0:HD] = dk
        out_ref[:, :, HD : 2 * HD] = dv


def join(is_light, held, mine, came):
    part = pl.BlockSpec((CHIPS, HALF, 2 * HD), lambda i: (0, 0, 0))
    if is_light:
        out_spec = pl.BlockSpec((SHARE, CHIPS, 16, HD), lambda i: (0, 0, HALF // 16, 0))
    else:
        out_spec = pl.BlockSpec((CHIPS, HALF, 2 * HD), lambda i: (0, 0, WIDTH // (2 * HD)))
    return pl.pallas_call(
        functools.partial(join_kernel, is_light),
        out_shape=jax.ShapeDtypeStruct(held.shape, held.dtype),
        grid=(1,),
        in_specs=[pl.BlockSpec(memory_space=pl.ANY), part, part],
        out_specs=out_spec,
        input_output_aliases={0: 0},
        cost_estimate=pl.CostEstimate(flops=0, bytes_accessed=2 << 20, transcendentals=0),
        name="join_light" if is_light else "join_heavy",
    )(held, mine, came)


def order_kernel(meta, in_ref, out_ref):
    out_ref[...] = in_ref[...]


def order(meta, arrived):
    spec = (1, CHIPS, HALF + 16, HD)
    return pl.pallas_call(
        order_kernel,
        out_shape=jax.ShapeDtypeStruct(arrived.shape, arrived.dtype),
        grid_spec=pltpu.PrefetchScalarGridSpec(
            num_scalar_prefetch=1,
            grid=(8,),
            in_specs=[pl.BlockSpec(spec, lambda d, meta: (source_of(meta, d), 0, 0, 0))],
            out_specs=pl.BlockSpec(spec, lambda d, meta: (d, 0, 0, 0)),
        ),
        cost_estimate=pl.CostEstimate(flops=0, bytes_accessed=3 << 20, transcendentals=0),
        name="order",
    )(meta, arrived)


def place_kernel(meta, heavy_ref, light_ref, dq_ref, dk_ref, dv_ref, hot):
    @pl.when(pl.program_id(0) == 0)
    def _():
        group = meta[ME]
        row = lax.broadcasted_iota(jnp.int32, (2 * HALF, 2 * HALF), 0)
        col = lax.broadcasted_iota(jnp.int32, (2 * HALF, 2 * HALF), 1)
        source = source_of(meta, group)
        taken = jnp.full((2 * HALF, 2 * HALF), -1, jnp.int32)
        for other in (False, True):
            if other:
                origin, half = source, light_half(meta, source)
            else:
                origin, half = group, 1 - light_half(meta, group)
            for i in range(4):
                e = (origin * 2 + half) * 4 + i
                begin = meta[TOFF + e] // 16
                length = meta[LEN + e] // 16
                from_row = meta[SRC + e] // 16 - half * HALF + (HALF if other else 0)
                inside = (row >= begin) & (row < begin + length)
                taken = jnp.where(inside, row - begin + from_row, taken)
        hot[...] = jnp.where(taken == col, 1.0, 0.0).astype(jnp.bfloat16)

    def put(rows):
        return jnp.dot(hot[...], rows, preferred_element_type=jnp.float32).astype(jnp.bfloat16)

    for j in range(SHARE):
        cols = slice(j * HD, (j + 1) * HD)
        dq_ref[:, cols] = put(
            jnp.concatenate([heavy_ref[0, :, cols], light_ref[j, 0, 0:HALF, :]], axis=0)
        )
    for which, out_ref in enumerate((dk_ref, dv_ref)):
        begin = WIDTH + which * HD
        pieces = [light_ref[4 * which + j, 0, HALF : HALF + 16, :] for j in range(4)]
        out_ref[...] = put(
            jnp.concatenate([heavy_ref[0, :, begin : begin + HD]] + pieces, axis=0)
        )


def place(meta, heavy, light):
    rows = 2 * HALF
    return pl.pallas_call(
        place_kernel,
        out_shape=(
            jax.ShapeDtypeStruct((rows, QH * HD), jnp.bfloat16),
            jax.ShapeDtypeStruct((rows, KVH * HD), jnp.bfloat16),
            jax.ShapeDtypeStruct((rows, KVH * HD), jnp.bfloat16),
        ),
        grid_spec=pltpu.PrefetchScalarGridSpec(
            num_scalar_prefetch=1,
            grid=(CHIPS,),
            in_specs=[
                pl.BlockSpec((1, HALF, WIDTH + 2 * HD), lambda m, meta: (m, 0, 0)),
                pl.BlockSpec((SHARE, 1, HALF + 16, HD), lambda m, meta: (0, m, 0, 0)),
            ],
            out_specs=(
                pl.BlockSpec((rows, WIDTH), lambda m, meta: (0, m)),
                pl.BlockSpec((rows, HD), lambda m, meta: (0, m)),
                pl.BlockSpec((rows, HD), lambda m, meta: (0, m)),
            ),
            scratch_shapes=[pltpu.VMEM((rows, rows), jnp.bfloat16)],
        ),
        cost_estimate=pl.CostEstimate(flops=1 << 28, bytes_accessed=5 << 20, transcendentals=0),
        name="place",
    )(meta, heavy, light)


def local(
    query_rows,
    key_rows,
    value_rows,
    grad_out,
    doc_length,
    source_group,
    source_offset,
    target_group,
    target_offset,
):
    dp_size = lax.axis_size("dp")
    seq_size = lax.axis_size("seq")
    rows = query_rows.shape[2]
    ids = jnp.stack([lax.axis_index("dp"), lax.axis_index("seq")]).astype(jnp.int32)
    meta = jnp.concatenate([doc_length, source_offset, target_group, target_offset, ids])
    chips = [[2 * m + c for m in range(CHIPS)] for c in range(2)]
    spread = [
        [d * seq_size + 2 * m + c for d in range(dp_size) for m in range(CHIPS)] for c in range(2)
    ]
    swap = [(i, i ^ 1) for i in range(seq_size)]

    first, second = pack(
        meta,
        query_rows.reshape(rows, QH * HD),
        grad_out.reshape(rows, QH * HD),
        key_rows.reshape(rows, KVH * HD),
        value_rows.reshape(rows, KVH * HD),
    )
    first = lax.all_to_all(first, "seq", 0, 0, tiled=True, axis_index_groups=chips)
    second = lax.all_to_all(second, "seq", 0, 0, tiled=True, axis_index_groups=chips)
    others = lax.ppermute(first[:, :, 2 * WIDTH :], "seq", swap)

    light, mine, give = attend(meta, True, first, first, 8, others, 0)
    came = lax.ppermute(give, "seq", swap)
    light = join(True, light, mine, came)
    light = lax.all_to_all(
        light.reshape(dp_size * CHIPS, HALF + 16, HD),
        ("dp", "seq"),
        0,
        0,
        tiled=True,
        axis_index_groups=spread,
    )
    light = order(meta, light.reshape(dp_size, CHIPS, HALF + 16, HD))
    light = lax.all_to_all(light, "dp", 0, 0, tiled=True)

    heavy, mine, give = attend(meta, False, second, first, 9, others, 1)
    came = lax.ppermute(give, "seq", swap)
    heavy = join(False, heavy, mine, came)
    heavy = lax.all_to_all(heavy, "seq", 0, 0, tiled=True, axis_index_groups=chips)

    dq, dk, dv = place(meta, heavy, light)
    shape = (1, 1, rows)
    return (
        dq.reshape(*shape, QH * HD),
        dk.reshape(*shape, KVH * HD),
        dv.reshape(*shape, KVH * HD),
    )


def solution(mesh):
    split = P("dp", "seq", None, None)
    return jax.shard_map(
        local,
        mesh=mesh,
        in_specs=(split,) * 4 + (P(),) * 5,
        out_specs=(split,) * 3,
        check_vma=False,
    )
```

```python
import functools
import math

import jax
import jax.numpy as jnp
from jax import lax
from jax.experimental import pallas as pl
from jax.experimental.pallas import tpu as pltpu
from jax.sharding import PartitionSpec as P

QH = 64
KVH = 8
HD = 128
SHARE = QH // KVH
HALF = 64
TILE = 16
CHIPS = 8
WIDTH = SHARE * HD
INV_ROOT = 1.0 / math.sqrt(HD)
LOG2E = 1.4426950408889634
VMEM = 64 * 1024 * 1024
IN_HBM = pl.BlockSpec(memory_space=pltpu.HBM)

LEN, SRC, TGT, TOFF, ME = 0, 64, 128, 192, 256


def light_half(meta, group):
    stays = jnp.int32(0)
    for i in range(4):
        e = group * 8 + i
        stays = stays | ((meta[LEN + e] > 0) & (meta[TGT + e] == group)).astype(jnp.int32)
    return stays


def half_target(meta, group, half):
    target = jnp.int32(0)
    for i in range(4):
        e = group * 8 + half * 4 + i
        target = jnp.maximum(target, jnp.where(meta[LEN + e] > 0, meta[TGT + e], 0))
    return target


def source_of(meta, group):
    found = jnp.int32(0)
    for other in range(8):
        goes = half_target(meta, other, light_half(meta, other))
        found = found + jnp.where(goes == group, other, 0)
    return found


def pack_kernel(parts, meta, *refs):
    count = len(parts)
    ins, out_ref = refs[:count], refs[count]
    buffer, in_sem, out_sem = refs[count + 1 :]
    light = light_half(meta, meta[ME])
    incoming = []
    for m in range(CHIPS):
        copies, base = [], 0
        for (is_light, width), ref in zip(parts, ins):
            half = light if is_light else 1 - light
            rows = pl.ds(pl.multiple_of(half * HALF, HALF), HALF)
            copies.append(
                pltpu.make_async_copy(
                    ref.at[rows, m * width : (m + 1) * width],
                    buffer.at[m, :, base : base + width],
                    in_sem.at[m],
                )
            )
            base += width
        for copy in copies:
            copy.start()
        incoming.append(copies)
    outgoing = []
    for m in range(CHIPS):
        for copy in incoming[m]:
            copy.wait()
        copy = pltpu.make_async_copy(buffer.at[m], out_ref.at[m], out_sem)
        copy.start()
        outgoing.append(copy)
    for copy in outgoing:
        copy.wait()


def pack(meta, name, *arrays):
    parts = tuple((is_light, array.shape[1] // CHIPS) for is_light, array in arrays)
    shape = (CHIPS, HALF, sum(width for _, width in parts))
    return pl.pallas_call(
        functools.partial(pack_kernel, parts),
        out_shape=jax.ShapeDtypeStruct(shape, jnp.bfloat16),
        grid_spec=pltpu.PrefetchScalarGridSpec(
            num_scalar_prefetch=1,
            grid=(),
            in_specs=[IN_HBM] * len(parts),
            out_specs=IN_HBM,
            scratch_shapes=[
                pltpu.VMEM(shape, jnp.bfloat16),
                pltpu.SemaphoreType.DMA((CHIPS,)),
                pltpu.SemaphoreType.DMA,
            ],
        ),
        compiler_params=pltpu.CompilerParams(vmem_limit_bytes=VMEM),
        cost_estimate=pl.CostEstimate(flops=0, bytes_accessed=10 << 20, transcendentals=0),
        name=name,
    )(meta, *[array for _, array in arrays])


def pick_kernel(rows_ref, after_ref, out_ref, buffer, sem):
    copy = pltpu.make_async_copy(rows_ref.at[:, :, 2 * WIDTH :], buffer, sem)
    copy.start()
    copy.wait()
    copy = pltpu.make_async_copy(buffer, out_ref, sem)
    copy.start()
    copy.wait()


def pick(rows, after):
    shape = (CHIPS, HALF, rows.shape[2] - 2 * WIDTH)
    return pl.pallas_call(
        pick_kernel,
        out_shape=jax.ShapeDtypeStruct(shape, rows.dtype),
        in_specs=[IN_HBM] * 2,
        out_specs=IN_HBM,
        scratch_shapes=[pltpu.VMEM(shape, rows.dtype), pltpu.SemaphoreType.DMA],
        compiler_params=pltpu.CompilerParams(vmem_limit_bytes=VMEM),
        cost_estimate=pl.CostEstimate(flops=0, bytes_accessed=1 << 20, transcendentals=0),
        name="pick",
    )(rows, after)


def attend_kernel(
    is_light,
    own_at,
    other_at,
    meta,
    rows_ref,
    own_in,
    other_in,
    *refs,
):
    count = 1 if is_light else CHIPS
    dq_outs, own_out, other_out = refs[:count], refs[count], refs[count + 1]
    dq_ref, rows_in, own_ref, other_ref, k_all, v_all, sem = refs[count + 2 :]
    copies = [
        pltpu.make_async_copy(own_in.at[:, :, own_at : own_at + 2 * HD], own_ref, sem.at[0]),
        pltpu.make_async_copy(other_in.at[:, :, other_at : other_at + 2 * HD], other_ref, sem.at[0]),
        pltpu.make_async_copy(rows_ref.at[:, :, 0 : 2 * WIDTH], rows_in, sem.at[1]),
    ]
    for copy in copies:
        copy.start()
    for copy in copies:
        copy.wait()
    group = meta[ME]
    core = meta[ME + 1] % 2
    half = light_half(meta, group)
    if not is_light:
        half = 1 - half
    k_all[0:CHIPS] = own_ref[:, :, 0:HD]
    k_all[CHIPS : 2 * CHIPS] = other_ref[:, :, 0:HD]
    v_all[0:CHIPS] = own_ref[:, :, HD : 2 * HD]
    v_all[CHIPS : 2 * CHIPS] = other_ref[:, :, HD : 2 * HD]
    own_out[...] = jnp.zeros_like(own_out)
    other_out[...] = jnp.zeros_like(other_out)
    queries = CHIPS * TILE
    nt = (((1,), (1,)), ((), ()))
    tn = (((0,), (0,)), ((), ()))

    def heads_of(which, first):
        pieces = []
        for h in range(SHARE):
            base = which * WIDTH + h * HD
            piece = rows_in[:, first : first + TILE, base : base + HD]
            pieces.append(piece.reshape(queries, HD))
        return jnp.concatenate(pieces, axis=0)

    for tile in range(HALF // TILE):
        first, rows = tile * TILE, (tile + 1) * TILE
        seen = 2 * CHIPS * rows
        lane = lax.broadcasted_iota(jnp.int32, (1, queries), 1)
        row_q = lane % TILE + first
        pos_q = row_q * 16 + 2 * (lane // TILE) + core
        start_q = jnp.zeros((1, queries), jnp.int32)
        for i in range(4):
            e = (group * 2 + half) * 4 + i
            length = meta[LEN + e]
            begin = meta[SRC + e] - half * (HALF * 16)
            inside = (row_q * 16 >= begin) & (row_q * 16 < begin + length)
            start_q = jnp.where(inside, begin, start_q)
        sub = lax.broadcasted_iota(jnp.int32, (seen, 1), 0)
        slot = sub // rows
        lane_k = jnp.where(slot < CHIPS, 2 * slot + core, 2 * (slot - CHIPS) + 1 - core)
        pos_k = (sub % rows) * 16 + lane_k
        allowed = (pos_k >= start_q) & (pos_k <= pos_q)
        bias = jnp.where(allowed, 0.0, -1e30)
        bias = jnp.concatenate([bias] * SHARE, axis=1)

        q = heads_of(0, first)
        g = heads_of(1, first)
        k = k_all[:, 0:rows, :].reshape(seen, HD)
        v = v_all[:, 0:rows, :].reshape(seen, HD)
        scores = lax.dot_general(k, q, nt, preferred_element_type=jnp.float32)
        dprobs = lax.dot_general(v, g, nt, preferred_element_type=jnp.float32)
        scores = scores * (INV_ROOT * LOG2E) + bias
        top = jnp.max(scores, axis=0, keepdims=True)
        weights = jnp.exp2(scores - top)
        recip = 1.0 / jnp.sum(weights, axis=0, keepdims=True)
        delta = jnp.sum(weights * dprobs, axis=0, keepdims=True) * recip
        soft = weights * recip
        low = soft.astype(jnp.bfloat16)
        dscores = (soft * (dprobs - delta)).astype(jnp.bfloat16)
        dv = jnp.dot(low, g, preferred_element_type=jnp.float32).reshape(2 * CHIPS, rows, HD)
        dk = jnp.dot(dscores, q, preferred_element_type=jnp.float32).reshape(2 * CHIPS, rows, HD)
        own_out[:, 0:rows, 0:HD] += dk[0:CHIPS]
        own_out[:, 0:rows, HD : 2 * HD] += dv[0:CHIPS]
        other_out[:, 0:rows, 0:HD] += dk[CHIPS : 2 * CHIPS]
        other_out[:, 0:rows, HD : 2 * HD] += dv[CHIPS : 2 * CHIPS]
        dq = lax.dot_general(dscores, k, tn, preferred_element_type=jnp.float32) * INV_ROOT
        dq = dq.astype(jnp.bfloat16).reshape(SHARE, CHIPS, TILE, HD)
        for h in range(SHARE):
            if is_light:
                dq_ref[h, :, first : first + TILE, :] = dq[h]
            else:
                dq_ref[:, first : first + TILE, h * HD : (h + 1) * HD] = dq[h]

    if is_light:
        copies = [pltpu.make_async_copy(dq_ref, dq_outs[0].at[:, :, 0:HALF], sem.at[0])]
    else:
        chip = meta[ME + 1] // 2
        copies = [
            pltpu.make_async_copy(dq_ref.at[chip ^ n], dq_outs[n].at[:, 0:WIDTH], sem.at[0])
            for n in range(CHIPS)
        ]
    for copy in copies:
        copy.start()
    for copy in copies:
        copy.wait()


def attend(meta, is_light, rows, own, own_at, other, other_at):
    part = pl.BlockSpec((CHIPS, HALF, 2 * HD), lambda i, meta: (0, 0, 0))
    if is_light:
        count, room = 1, (SHARE, CHIPS, HALF + 16, HD)
        dq_shape = (SHARE, CHIPS, HALF, HD)
    else:
        count, room = CHIPS, (HALF, WIDTH + 2 * HD)
        dq_shape = (CHIPS, HALF, WIDTH)
    out = pl.pallas_call(
        functools.partial(attend_kernel, is_light, own_at, other_at),
        out_shape=(jax.ShapeDtypeStruct(room, jnp.bfloat16),) * count
        + (jax.ShapeDtypeStruct((CHIPS, HALF, 2 * HD), jnp.float32),) * 2,
        grid_spec=pltpu.PrefetchScalarGridSpec(
            num_scalar_prefetch=1,
            grid=(1,),
            in_specs=[IN_HBM] * 3,
            out_specs=(IN_HBM,) * count + (part, part),
            scratch_shapes=[
                pltpu.VMEM(dq_shape, jnp.bfloat16),
                pltpu.VMEM((CHIPS, HALF, 2 * WIDTH), jnp.bfloat16),
                pltpu.VMEM((CHIPS, HALF, 2 * HD), jnp.bfloat16),
                pltpu.VMEM((CHIPS, HALF, 2 * HD), jnp.bfloat16),
                pltpu.VMEM((2 * CHIPS, HALF, HD), jnp.bfloat16),
                pltpu.VMEM((2 * CHIPS, HALF, HD), jnp.bfloat16),
                pltpu.SemaphoreType.DMA((2,)),
            ],
        ),
        compiler_params=pltpu.CompilerParams(vmem_limit_bytes=VMEM),
        cost_estimate=pl.CostEstimate(
            flops=8 << 30, bytes_accessed=6 << 20, transcendentals=3 << 20
        ),
        name="attend_light" if is_light else "attend_heavy",
    )(meta, rows, own, other)
    return out[:count], out[count], out[count + 1]


def summed(mine_ref, came_ref):
    total = mine_ref[...] + came_ref[...]
    dk = (total[:, :, 0:HD] * INV_ROOT).astype(jnp.bfloat16)
    return dk, total[:, :, HD : 2 * HD].astype(jnp.bfloat16)


def join_light_kernel(held_ref, mine_ref, came_ref, out_ref):
    dk, dv = summed(mine_ref, came_ref)
    for j in range(4):
        out_ref[j] = dk[:, 16 * j : 16 * j + 16, :]
        out_ref[4 + j] = dv[:, 16 * j : 16 * j + 16, :]


def join_light(held, mine, came):
    part = pl.BlockSpec((CHIPS, HALF, 2 * HD), lambda i: (0, 0, 0))
    return pl.pallas_call(
        join_light_kernel,
        out_shape=jax.ShapeDtypeStruct(held.shape, held.dtype),
        grid=(1,),
        in_specs=[IN_HBM, part, part],
        out_specs=pl.BlockSpec((SHARE, CHIPS, 16, HD), lambda i: (0, 0, HALF // 16, 0)),
        input_output_aliases={0: 0},
        cost_estimate=pl.CostEstimate(flops=0, bytes_accessed=2 << 20, transcendentals=0),
        name="join_light",
    )(held, mine, came)


def join_heavy_kernel(meta, mine_ref, came_ref, *refs):
    outs = refs[CHIPS : 2 * CHIPS]
    buffer, sem = refs[2 * CHIPS :]
    dk, dv = summed(mine_ref, came_ref)
    buffer[:, :, 0:HD] = dk
    buffer[:, :, HD : 2 * HD] = dv
    chip = meta[ME + 1] // 2
    copies = [
        pltpu.make_async_copy(buffer.at[chip ^ n], outs[n].at[:, WIDTH : WIDTH + 2 * HD], sem)
        for n in range(CHIPS)
    ]
    for copy in copies:
        copy.start()
    for copy in copies:
        copy.wait()


def join_heavy(meta, held, mine, came):
    part = pl.BlockSpec((CHIPS, HALF, 2 * HD), lambda i, meta: (0, 0, 0))
    return pl.pallas_call(
        join_heavy_kernel,
        out_shape=tuple(jax.ShapeDtypeStruct(x.shape, x.dtype) for x in held),
        grid_spec=pltpu.PrefetchScalarGridSpec(
            num_scalar_prefetch=1,
            grid=(1,),
            in_specs=[part, part] + [IN_HBM] * CHIPS,
            out_specs=(IN_HBM,) * CHIPS,
            scratch_shapes=[
                pltpu.VMEM((CHIPS, HALF, 2 * HD), held[0].dtype),
                pltpu.SemaphoreType.DMA,
            ],
        ),
        input_output_aliases={3 + n: n for n in range(CHIPS)},
        cost_estimate=pl.CostEstimate(flops=0, bytes_accessed=2 << 20, transcendentals=0),
        name="join_heavy",
    )(meta, mine, came, *held)


def order_kernel(meta, in_ref, after_ref, out_ref, buffer, in_sem, out_sem):
    incoming = []
    for origin in range(8):
        copy = pltpu.make_async_copy(in_ref.at[origin], buffer.at[origin], in_sem.at[origin])
        copy.start()
        incoming.append(copy)
    outgoing = []
    for origin, copy in enumerate(incoming):
        target = half_target(meta, origin, light_half(meta, origin))
        copy.wait()
        copy = pltpu.make_async_copy(buffer.at[origin], out_ref.at[target], out_sem)
        copy.start()
        outgoing.append(copy)
    for copy in outgoing:
        copy.wait()


def order(meta, arrived, after):
    return pl.pallas_call(
        order_kernel,
        out_shape=jax.ShapeDtypeStruct(arrived.shape, arrived.dtype),
        grid_spec=pltpu.PrefetchScalarGridSpec(
            num_scalar_prefetch=1,
            grid=(),
            in_specs=[IN_HBM] * 2,
            out_specs=IN_HBM,
            scratch_shapes=[
                pltpu.VMEM(arrived.shape, arrived.dtype),
                pltpu.SemaphoreType.DMA((8,)),
                pltpu.SemaphoreType.DMA,
            ],
        ),
        compiler_params=pltpu.CompilerParams(vmem_limit_bytes=VMEM),
        cost_estimate=pl.CostEstimate(flops=0, bytes_accessed=3 << 20, transcendentals=0),
        name="order",
    )(meta, arrived, after)


def place_kernel(meta, *refs):
    heavies, light_ref, outs = refs[:CHIPS], refs[CHIPS], refs[CHIPS + 1 : CHIPS + 4]
    heavy, light, dq, dk, dv, hot, in_sem, out_sem = refs[CHIPS + 4 :]
    chip = meta[ME + 1] // 2
    incoming = []
    for n in range(CHIPS):
        m = chip ^ n
        copies = [
            pltpu.make_async_copy(heavies[n], heavy.at[n], in_sem.at[n]),
            pltpu.make_async_copy(light_ref.at[:, m], light.at[:, n], in_sem.at[n]),
        ]
        for copy in copies:
            copy.start()
        incoming.append(copies)

    group = meta[ME]
    row = lax.broadcasted_iota(jnp.int32, (2 * HALF, 2 * HALF), 0)
    col = lax.broadcasted_iota(jnp.int32, (2 * HALF, 2 * HALF), 1)
    source = source_of(meta, group)
    taken = jnp.full((2 * HALF, 2 * HALF), -1, jnp.int32)
    for other in (False, True):
        if other:
            origin, half = source, light_half(meta, source)
        else:
            origin, half = group, 1 - light_half(meta, group)
        for i in range(4):
            e = (origin * 2 + half) * 4 + i
            begin = meta[TOFF + e] // 16
            length = meta[LEN + e] // 16
            from_row = meta[SRC + e] // 16 - half * HALF + (HALF if other else 0)
            inside = (row >= begin) & (row < begin + length)
            taken = jnp.where(inside, row - begin + from_row, taken)
    hot[...] = jnp.where(taken == col, 1.0, 0.0).astype(jnp.bfloat16)

    def put(rows):
        return jnp.dot(hot[...], rows, preferred_element_type=jnp.float32).astype(jnp.bfloat16)

    outgoing = []
    for n in range(CHIPS):
        m = chip ^ n
        for copy in incoming[n]:
            copy.wait()
        wide = jnp.concatenate([light[j, n, 0:HALF, :] for j in range(SHARE)], axis=1)
        dq[n] = put(jnp.concatenate([heavy[n, :, 0:WIDTH], wide], axis=0))
        for which, buffer in enumerate((dk, dv)):
            begin = WIDTH + which * HD
            pieces = [light[4 * which + j, n, HALF : HALF + 16, :] for j in range(4)]
            buffer[n] = put(
                jnp.concatenate([heavy[n, :, begin : begin + HD]] + pieces, axis=0)
            )
        for buffer, out_ref, width in zip((dq, dk, dv), outs, (WIDTH, HD, HD)):
            columns = pl.ds(pl.multiple_of(m * width, width), width)
            copy = pltpu.make_async_copy(buffer.at[n], out_ref.at[:, columns], out_sem)
            copy.start()
            outgoing.append(copy)
    for copy in outgoing:
        copy.wait()


def place(meta, heavies, light):
    rows = 2 * HALF
    return pl.pallas_call(
        place_kernel,
        out_shape=(
            jax.ShapeDtypeStruct((rows, QH * HD), jnp.bfloat16),
            jax.ShapeDtypeStruct((rows, KVH * HD), jnp.bfloat16),
            jax.ShapeDtypeStruct((rows, KVH * HD), jnp.bfloat16),
        ),
        grid_spec=pltpu.PrefetchScalarGridSpec(
            num_scalar_prefetch=1,
            grid=(),
            in_specs=[IN_HBM] * (CHIPS + 1),
            out_specs=(IN_HBM,) * 3,
            scratch_shapes=[
                pltpu.VMEM((CHIPS, HALF, WIDTH + 2 * HD), jnp.bfloat16),
                pltpu.VMEM((SHARE, CHIPS, HALF + 16, HD), jnp.bfloat16),
                pltpu.VMEM((CHIPS, rows, WIDTH), jnp.bfloat16),
                pltpu.VMEM((CHIPS, rows, HD), jnp.bfloat16),
                pltpu.VMEM((CHIPS, rows, HD), jnp.bfloat16),
                pltpu.VMEM((rows, rows), jnp.bfloat16),
                pltpu.SemaphoreType.DMA((CHIPS,)),
                pltpu.SemaphoreType.DMA,
            ],
        ),
        compiler_params=pltpu.CompilerParams(vmem_limit_bytes=VMEM),
        cost_estimate=pl.CostEstimate(flops=1 << 28, bytes_accessed=5 << 20, transcendentals=0),
        name="place",
    )(meta, *heavies, light)


def local(
    query_rows,
    key_rows,
    value_rows,
    grad_out,
    doc_length,
    source_group,
    source_offset,
    target_group,
    target_offset,
):
    dp_size = lax.axis_size("dp")
    seq_size = lax.axis_size("seq")
    rows = query_rows.shape[2]
    ids = jnp.stack([lax.axis_index("dp"), lax.axis_index("seq")]).astype(jnp.int32)
    meta = jnp.concatenate([doc_length, source_offset, target_group, target_offset, ids])
    chips = [[2 * m + c for m in range(CHIPS)] for c in range(2)]
    spread = [
        [d * seq_size + 2 * m + c for d in range(dp_size) for m in range(CHIPS)] for c in range(2)
    ]
    swap = [(i, i ^ 1) for i in range(seq_size)]

    query = query_rows.reshape(rows, QH * HD)
    grad = grad_out.reshape(rows, QH * HD)
    key = key_rows.reshape(rows, KVH * HD)
    value = value_rows.reshape(rows, KVH * HD)

    def exchange(slots):
        return [
            slots[n]
            if n == 0
            else lax.ppermute(slots[n], "seq", [(i, i ^ (2 * n)) for i in range(seq_size)])
            for n in range(CHIPS)
        ]

    first = pack(
        meta,
        "pack_light",
        (True, query),
        (True, grad),
        (True, key),
        (True, value),
        (False, key),
        (False, value),
    )
    second_out = pack(meta, "pack_heavy", (False, query), (False, grad))
    first = lax.all_to_all(first, "seq", 0, 0, tiled=True, axis_index_groups=chips)
    second = lax.all_to_all(second_out, "seq", 0, 0, tiled=True, axis_index_groups=chips)
    base = 2 * WIDTH
    others = lax.ppermute(pick(first, second_out), "seq", swap)

    (light,), mine, give = attend(meta, True, first, first, base, others, 0)
    came = lax.ppermute(give, "seq", swap)
    light = join_light(light, mine, came)
    light = lax.all_to_all(
        light.reshape(dp_size * CHIPS, HALF + 16, HD),
        ("dp", "seq"),
        0,
        0,
        tiled=True,
        axis_index_groups=spread,
    )
    light = light.reshape(dp_size, CHIPS, HALF + 16, HD)

    heavy, mine, give = attend(meta, False, second, first, base + 2 * HD, others, 2 * HD)
    came = lax.ppermute(give, "seq", swap)
    heavy = join_heavy(meta, heavy, mine, came)
    light = order(meta, light, heavy[0])
    light = lax.all_to_all(light, "dp", 0, 0, tiled=True)
    heavy = exchange(heavy)

    dq, dk, dv = place(meta, heavy, light)
    shape = (1, 1, rows)
    return (
        dq.reshape(*shape, QH * HD),
        dk.reshape(*shape, KVH * HD),
        dv.reshape(*shape, KVH * HD),
    )


def solution(mesh):
    split = P("dp", "seq", None, None)
    return jax.shard_map(
        local,
        mesh=mesh,
        in_specs=(split,) * 4 + (P(),) * 5,
        out_specs=(split,) * 3,
        check_vma=False,
    )
```
